32 devices in a mesh: grp: 2 (over x), lon: 16 (over z, y, core).
Axes of the slice: x: 2, y: 2, z: 4, core: 2. Of those that a mesh axis runs over, the one named last changes fastest.
Arguments:
- field: bfloat16 [128, 256, 512], P('grp', 'lon'), parts along dimension 0, may hold values from -6 to 6
- cotangent: bfloat16 [128, 256, 512], P('grp', 'lon'), parts along dimension 0, may hold values from -6 to 6
- offsets: int32 [64], replicated, may hold values from 0 to 56, as said below
- widths: int32 [64], replicated, may hold values from 2 to 8
- kernel: bfloat16 [64, 8, 5, 3], replicated, may hold values from -1 to 1
- cycle: float32 [6, 8, 3], replicated, may hold values from -2 to 2
- mixing: bfloat16 [512, 3, 512], replicated, may hold values from -0.15625 to 0.15625
Outputs:
- output: bfloat16 [128, 256, 512], P('grp', 'lon'), parts along dimension 0
- field_grad: bfloat16 [128, 256, 512], P('grp', 'lon'), parts along dimension 0
- mixing_grad: float32 [512, 6, 512], P('lon', 'grp'), parts along dimension 1
The draws below stay inside these ranges and needn't reach their ends.
There are 2 independent parts, one for each index of `grp`. The reference program is written for one: setup_inputs(seed, part) draws one part's arguments, and reference() takes and returns one part's arrays. A program takes and returns all parts, laid end to end along the dimension named above; an argument that names none is the same for every part. Nothing has to cross between parts.
Inputs may be any that keep to these rules, and one draw needn't show every extreme that they name: offsets[i] + 8 <= 64; the polar rows i < 6 use all 8 rows.
All inputs are finite; a program needn't handle non-finite values.
Results may differ from the reference program's by a relative error of at most 0.0061.
Values may be sent and summed in bfloat16 or wider, within the bound.
A program may use at most 64 MiB of HBM per device.

```python
import jax
import jax.numpy as jnp
from jax import lax

C = 512
LAT = 64
BAND = 8
R = 2
K = 3
POLAR = 6
PB = 8
LON = 256


def band_tables(key):
    first, second = jax.random.split(key)
    rows = jnp.arange(LAT, dtype=jnp.int32)
    loose = jax.random.randint(first, (LAT,), 2, BAND + 1).astype(jnp.int32)
    widths = jnp.where(rows < POLAR, BAND, loose).astype(jnp.int32)
    jitter = jax.random.randint(second, (LAT,), -1, 2).astype(jnp.int32)
    offsets = jnp.clip(rows - widths // 2 + jitter, 0, LAT - BAND).astype(jnp.int32)
    return (offsets, widths)


def draw_offsets(key, part):
    offsets, widths = band_tables(key)
    return offsets


def draw_widths(key, part):
    offsets, widths = band_tables(key)
    return widths


def levels(stream_key, extent, pieces, least, high):
    gain = 1.0
    for position, blocks in pieces:
        draws = jax.random.uniform(jax.random.fold_in(jax.random.fold_in(stream_key, 6), position), (blocks,), jnp.float32, least / len(pieces), high / len(pieces))
        gain = gain * jnp.repeat(jnp.exp(draws), extent[position] // blocks).reshape((-1,) + (1,) * (len(extent) - 1 - position))
    return gain


def noise(key, shape, scale, reach, cuts=(), kind=jnp.bfloat16):
    values = jax.random.normal(key, shape, jnp.float32) * scale
    if len(cuts) > 0:
        values = levels(key, shape, cuts, -0.22, 0.18) * values
    return jnp.clip(values, min=-reach, max=reach).astype(kind)


def setup_inputs(seed: int = 0, part: int = 0) -> dict:
    seeds = jax.random.split(jax.random.key(seed), 8)
    own_keys = jax.random.split(jax.random.fold_in(seeds[7], part), 8)
    field = noise(own_keys[0], (LAT, LON, C), 1.0, 6.0, ((1, 16),))
    cotangent = noise(own_keys[1], (LAT, LON, C), 1.0, 6.0, ((1, 16),))
    offsets = draw_offsets(jax.random.fold_in(seeds[7], 71), part)
    widths = draw_widths(jax.random.fold_in(seeds[7], 71), part)
    kernel = noise(seeds[4], (LAT, BAND, 2 * R + 1, K), (BAND * (2 * R + 1)) ** -0.5, 1.0)
    cycle = noise(seeds[5], (POLAR, PB, K), PB ** -0.5, 2.0, (), jnp.float32)
    mixing = noise(seeds[6], (C, K, C), (K * C) ** -0.5, 0.15625)
    return {"field": field, "cotangent": cotangent, "offsets": offsets, "widths": widths, "kernel": kernel, "cycle": cycle, "mixing": mixing}


def silu_slope(mixed):
    sig = jax.nn.sigmoid(mixed)
    return sig * (1.0 + mixed * (1.0 - sig))


def reference(field, cotangent, offsets, widths, kernel, cycle, mixing):
    lon_all = field.shape[1]
    scale = float(lon_all) ** -0.5
    keep = (jnp.arange(BAND, dtype=jnp.int32)[None, :] < widths[:, None]).astype(jnp.float32)
    band = kernel.astype(jnp.float32) * keep[:, :, None, None]
    wrapped = jnp.concatenate([field[:, lon_all - R:], field, field[:, :R]], axis=1).astype(jnp.float32)
    conv = jnp.zeros((LAT, lon_all, K, C), jnp.float32)
    for b in range(BAND):
        picked = jnp.take(wrapped, (offsets + b).astype(jnp.int32), axis=0)
        for t in range(2 * R + 1):
            conv = conv + jnp.einsum('ik,ijc->ijkc', band[:, b, t, :], picked[:, t:t + lon_all])
    zonal = jnp.sum(field[:PB].astype(jnp.float32), axis=1) * scale
    cycle_term = jnp.einsum('ipk,pc->ikc', cycle, zonal, precision=lax.Precision.HIGHEST)
    conv = conv.at[:POLAR].add(cycle_term[:, None])
    conv_b = conv.astype(jnp.bfloat16)
    mixed = jnp.einsum('ijkc,ckd->ijd', conv_b.astype(jnp.float32), mixing.astype(jnp.float32))
    output = jax.nn.silu(mixed).astype(jnp.bfloat16)
    mixed_grad = (cotangent.astype(jnp.float32) * silu_slope(mixed)).astype(jnp.bfloat16)
    mixing_grad = jnp.einsum('ijkc,ijd->ckd', conv_b.astype(jnp.float32), mixed_grad.astype(jnp.float32))
    conv_grad = jnp.einsum('ijd,ckd->ijkc', mixed_grad.astype(jnp.float32), mixing.astype(jnp.float32)).astype(jnp.bfloat16)
    grad_wrapped = jnp.concatenate([conv_grad[:, lon_all - R:], conv_grad, conv_grad[:, :R]], axis=1).astype(jnp.float32)
    field_grad = jnp.zeros((LAT, lon_all, C), jnp.float32)
    for b in range(BAND):
        contrib = jnp.zeros((LAT, lon_all, C), jnp.float32)
        for t in range(2 * R + 1):
            contrib = contrib + jnp.einsum('ik,ijkc->ijc', band[:, b, t, :], grad_wrapped[:, 2 * R - t:2 * R - t + lon_all])
        field_grad = field_grad + jax.ops.segment_sum(contrib, (offsets + b).astype(jnp.int32), num_segments=LAT)
    cycle_sums = jnp.sum(conv_grad[:POLAR].astype(jnp.float32), axis=1)
    zonal_grad = jnp.einsum('ipk,ikc->pc', cycle, cycle_sums, precision=lax.Precision.HIGHEST) * scale
    field_grad = field_grad.at[:PB].add(zonal_grad[:, None])
    return output, field_grad.astype(jnp.bfloat16), mixing_grad
```

```python
import functools

import jax
import jax.numpy as jnp
from jax import lax
from jax.experimental import pallas as pl
from jax.experimental.pallas import tpu as pltpu
from jax.sharding import PartitionSpec as P

BAND = 8
R = 2
TAPS = 2 * R + 1
K = 3
POLAR = 6
PB = 8
MESH = pl.DeviceIdType.MESH
F32 = jnp.float32
BF16 = jnp.bfloat16


def kernel_body(
    n,
    direct,
    scale,
    field,
    cot_hbm,
    mix_hbm,
    taps,
    offs,
    wids,
    cyc_f,
    cyc_b,
    out,
    fgrad,
    mgrad,
    xt,
    cot,
    mix,
    pieces,
    fwd,
    bwd,
    conv,
    polar,
    mg,
    cg,
    ms,
    zbuf,
    sbuf,
    part,
    partb,
    r1,
    s2,
    r2,
    in_sem,
    h_send,
    h_recv,
    g_send,
    g_recv,
    z_send,
    z_recv,
    s_send,
    s_recv,
    a_send,
    a_recv,
    b_send,
    b_recv,
):
    cols = field.shape[0]
    lat = field.shape[1]
    ch = field.shape[2]
    me = lax.axis_index("lon")
    right, left = lax.rem(me + 1, n), lax.rem(me + n - 1, n)

    barrier = pltpu.get_barrier_semaphore()

    def greet(d, carry):
        pl.semaphore_signal(
            barrier, inc=1, device_id={"lon": lax.rem(me + d, n)}, device_id_type=MESH
        )
        return carry

    lax.fori_loop(1, n, greet, 0)

    load_field = pltpu.make_async_copy(field, xt.at[pl.ds(R, cols)], in_sem.at[0])
    load_mix = pltpu.make_async_copy(mix_hbm, mix, in_sem.at[1])
    load_cot = pltpu.make_async_copy(cot_hbm, cot, in_sem.at[2])
    load_field.start()
    load_mix.start()
    load_cot.start()

    def remote(src, dst, send, recv, peer):
        return pltpu.make_async_remote_copy(
            src_ref=src,
            dst_ref=dst,
            send_sem=send,
            recv_sem=recv,
            device_id={"lon": peer},
            device_id_type=MESH,
        )

    def spread(buf, send, recv):
        def copy(d):
            return remote(buf.at[0], buf.at[d], send.at[d], recv.at[d], lax.rem(me + d, n))

        return copy

    def start_all(copy):
        def step(d, carry):
            copy(d).start()
            return carry

        lax.fori_loop(1, n, step, 0)

    def wait_all(copy):
        def step(d, carry):
            copy(d).wait()
            return carry

        lax.fori_loop(1, n, step, 0)

    pl.semaphore_wait(barrier, n - 1)
    halo_l = remote(
        field.at[pl.ds(0, R)], xt.at[pl.ds(R + cols, R)], h_send.at[0], h_recv.at[0], left
    )
    halo_r = remote(
        field.at[pl.ds(cols - R, R)], xt.at[pl.ds(0, R)], h_send.at[1], h_recv.at[1], right
    )
    halo_l.start()
    halo_r.start()
    load_field.wait()
    zbuf[0] = jnp.sum(xt[R : R + cols, 0:16, :].astype(F32), axis=0)[0:PB]
    zonal_copy = spread(zbuf, z_send, z_recv)
    start_all(zonal_copy)

    wide = 2 * K * lat
    rel = lax.broadcasted_iota(jnp.int32, (lat, wide), 0) - offs[...]
    used = rel < wids[...]
    for t in range(TAPS + 1):
        acc = jnp.zeros((lat, wide), F32)
        for b in range(BAND):
            row = taps[t * BAND + b : t * BAND + b + 1, :]
            acc = jnp.where((rel == b) & used, row, acc)
        pieces[t * lat : (t + 1) * lat, :] = acc
    fwd[...] = pieces[...].T.astype(BF16)
    for a in range(4):
        for p in range(4):
            t = 2 * R - 2 * p + a
            if 0 <= t <= TAPS:
                block = pieces[t * lat : (t + 1) * lat, :].astype(BF16)
            else:
                block = jnp.zeros((lat, wide), BF16)
            bwd[a * lat : (a + 1) * lat, p * wide : (p + 1) * wide] = block

    def conv_pair(p):
        source = xt[pl.ds(2 * p, TAPS + 1)].reshape((TAPS + 1) * lat, ch)
        c = jnp.dot(fwd[...], source, preferred_element_type=F32)
        c = c.reshape(2, K, lat, ch)
        polar[pl.ds(2 * p, 2)] = c[:, :, 0:16]
        conv[pl.ds(2 * p, 2)] = c.astype(BF16)

    def loop(lo, hi, fn):
        def step(i, carry):
            fn(i)
            return carry

        lax.fori_loop(lo, hi, step, 0)

    pairs = cols // 2
    loop(1, pairs - 1, conv_pair)
    halo_l.wait()
    halo_r.wait()
    loop(0, 2, lambda i: conv_pair(i * (pairs - 1)))

    wait_all(zonal_copy)
    zonal = jnp.sum(zbuf[...], axis=0) * scale
    term = jnp.zeros((K * 16, ch), F32)
    for p in range(PB):
        term = term + cyc_f[:, p : p + 1] * zonal[p : p + 1, :]
    term = term.reshape(1, K, 16, ch)
    load_mix.wait()
    load_cot.wait()
    ms[...] = jnp.zeros_like(ms)

    def mix_group(g):
        at = pl.ds(4 * g, 4)
        conv[at, :, 0:16] = (polar[at] + term).astype(BF16)
        mixed = jnp.dot(
            conv[at, 0].reshape(4 * lat, ch), mix[0], preferred_element_type=F32
        )
        for k in range(1, K):
            mixed = mixed + jnp.dot(
                conv[at, k].reshape(4 * lat, ch), mix[k], preferred_element_type=F32
            )
        sig = jax.nn.sigmoid(mixed)
        out[at] = (mixed * sig).astype(BF16).reshape(4, lat, ch)
        ct = cot[at].reshape(4 * lat, ch).astype(F32)
        grad = (ct * (sig * (1.0 + mixed * (1.0 - sig)))).astype(BF16).reshape(4, lat, ch)
        mg[pl.ds(R + 4 * g, 4)] = grad
        ms[...] += jnp.sum(grad[:, 0:16].astype(F32), axis=0)

    groups = cols // 4
    loop(0, 2, lambda i: mix_group(i * (groups - 1)))
    grad_l = remote(
        mg.at[pl.ds(R, R)], mg.at[pl.ds(R + cols, R)], g_send.at[0], g_recv.at[0], left
    )
    grad_r = remote(
        mg.at[pl.ds(cols, R)], mg.at[pl.ds(0, R)], g_send.at[1], g_recv.at[1], right
    )
    grad_l.start()
    grad_r.start()
    loop(1, groups - 1, mix_group)
    sbuf[0] = ms[0:PB]
    sums_copy = spread(sbuf, s_send, s_recv)
    start_all(sums_copy)

    half = ch // 2
    if direct:
        rows = ch // n
        chips = n // 2
        core = lax.rem(me, 2)
        chip = me // 2
        sibling = chip * 2 + (1 - core)
        per = half // (2 * rows)

        def pair_copy(k):
            return remote(
                partb.at[k, 1 - core], r1.at[k], a_send.at[k], a_recv.at[k], sibling
            )

        def chip_copy(k, d):
            return remote(
                s2.at[k, d],
                r2.at[k, d],
                b_send.at[k, d],
                b_recv.at[k, d],
                lax.rem(chip + d, chips) * 2 + core,
            )

        def pass_on(k):
            pair_copy(k).wait()

            def step(d):
                to = lax.rem(chip + d, chips)
                s2[k, d] = (part[k, core, to] + r1[k, to].astype(F32)).astype(BF16)
                chip_copy(k, d).start()

            loop(1, chips, step)

    for k in range(K):

        def product(h):
            lanes = pl.ds(pl.multiple_of(h * half, half), half)
            res = lax.dot_general(
                conv[:, k, :, lanes].reshape(cols * lat, half),
                mg[R : R + cols].reshape(cols * lat, ch),
                (((0,), (0,)), ((), ())),
                preferred_element_type=F32,
            )
            if not direct:
                mgrad[k, lanes, :] = res
                return
            res = res.reshape(per, 2, rows, ch)
            resb = res.astype(BF16)
            for c in range(2):
                part[k, c, pl.ds(h * per, per)] = res[:, c]
                partb[k, c, pl.ds(h * per, per)] = resb[:, c]

        loop(0, 2, product)
        if direct:
            pair_copy(k).start()
            if k > 0:
                pass_on(k - 1)
    if direct:
        pass_on(K - 1)

    def spread_grad(g):
        at = pl.ds(4 * g, 4)
        source = mg[at].reshape(4 * lat, ch)
        for k in range(K):
            res = lax.dot_general(
                source, mix[k], (((1,), (1,)), ((), ())), preferred_element_type=F32
            )
            cg[at, k] = res.astype(BF16).reshape(4, lat, ch)

    loop(1, groups, spread_grad)
    grad_l.wait()
    grad_r.wait()
    loop(0, 2, lambda i: spread_grad(i * groups))

    wait_all(sums_copy)
    total = jnp.sum(sbuf[...], axis=0)
    high = total.astype(BF16)
    low = (total - high.astype(F32)).astype(BF16)
    both = jnp.concatenate([high.astype(F32), low.astype(F32)], axis=0).astype(BF16)
    zgrad = jnp.zeros((PB, ch), F32)
    for k in range(K):
        res = lax.dot_general(
            both, mix[k], (((1,), (1,)), ((), ())), preferred_element_type=F32
        )
        res = res[0:PB] + res[PB : 2 * PB]
        for i in range(POLAR):
            at = k * POLAR + i
            zgrad = zgrad + cyc_b[:, at : at + 1] * res[i : i + 1, :]
    zgrad = zgrad * scale
    zgrad = jnp.concatenate([zgrad, jnp.zeros((16 - PB, ch), F32)], axis=0)[None]

    def field_group(g):
        at = pl.ds(4 * g, 4)
        source = cg[pl.ds(4 * g, 8)].reshape(8 * K * lat, ch)
        res = jnp.dot(bwd[...], source, preferred_element_type=F32).reshape(4, lat, ch)
        fgrad[at] = res.astype(BF16)
        fgrad[at, 0:16] = (res[:, 0:16] + zgrad).astype(BF16)

    loop(0, groups, field_group)

    if direct:
        for k in range(K):
            acc = part[k, core, chip] + r1[k, chip].astype(F32)
            for d in range(1, chips):
                chip_copy(k, d).wait()
                acc = acc + r2[k, d].astype(F32)
            mgrad[k] = acc


def body(n, field, cotangent, offsets, widths, kernel, cycle, mixing):
    lat, cols, ch = field.shape
    scale = float(cols * n) ** (-0.5)
    rows = ch // n
    direct = n % 2 == 0 and n > 2 and rows % 16 == 0
    field_t = jnp.swapaxes(field, 0, 1)
    cot_t = jnp.swapaxes(cotangent, 0, 1)
    mix_t = jnp.swapaxes(mixing, 0, 1)
    taps = jnp.transpose(kernel, (2, 1, 3, 0)).reshape(TAPS * BAND, K * lat).astype(F32)
    taps = jnp.concatenate(
        [jnp.pad(taps, ((0, BAND), (0, 0))), jnp.pad(taps, ((BAND, 0), (0, 0)))], axis=1
    )
    offs = jnp.tile(offsets, 2 * K)[None]
    wids = jnp.tile(widths, 2 * K)[None]
    cyc_f = jnp.pad(jnp.transpose(cycle, (2, 0, 1)), ((0, 0), (0, 16 - POLAR), (0, 0)))
    cyc_f = cyc_f.reshape(K * 16, PB)
    cyc_b = jnp.transpose(cycle, (1, 2, 0)).reshape(PB, K * POLAR)

    wide = 2 * K * lat
    dma = pltpu.SemaphoreType.DMA
    chips = n // 2 if direct else 1
    brows = rows if direct else 16
    vmem = pl.BlockSpec(memory_space=pltpu.VMEM)
    hbm = pl.BlockSpec(memory_space=pl.ANY)
    out_t, fgrad_t, mgrad_t = pl.pallas_call(
        functools.partial(kernel_body, n, direct, scale),
        out_shape=[
            jax.ShapeDtypeStruct((cols, lat, ch), BF16),
            jax.ShapeDtypeStruct((cols, lat, ch), BF16),
            jax.ShapeDtypeStruct((K, rows if direct else ch, ch), F32),
        ],
        in_specs=[hbm] * 3 + [vmem] * 5,
        out_specs=[vmem] * 3,
        scratch_shapes=[
            pltpu.VMEM((cols + 2 * R, lat, ch), BF16),
            pltpu.VMEM((cols, lat, ch), BF16),
            pltpu.VMEM((K, ch, ch), BF16),
            pltpu.VMEM(((TAPS + 1) * lat, wide), F32),
            pltpu.VMEM((wide, (TAPS + 1) * lat), BF16),
            pltpu.VMEM((4 * lat, 4 * wide), BF16),
            pltpu.VMEM((cols, K, lat, ch), BF16),
            pltpu.VMEM((cols, K, 16, ch), F32),
            pltpu.VMEM((cols + 2 * R, lat, ch), BF16),
            pltpu.VMEM((cols + 2 * R, K, lat, ch), BF16),
            pltpu.VMEM((16, ch), F32),
            pltpu.VMEM((n, PB, ch), F32),
            pltpu.VMEM((n, PB, ch), F32),
            pltpu.VMEM((K, 2, chips, brows, ch), F32),
            pltpu.VMEM((K, 2, chips, brows, ch), BF16),
            pltpu.VMEM((K, chips, brows, ch), BF16),
            pltpu.VMEM((K, chips, brows, ch), BF16),
            pltpu.VMEM((K, chips, brows, ch), BF16),
            dma((3,)),
            dma((2,)),
            dma((2,)),
            dma((2,)),
            dma((2,)),
            dma((n,)),
            dma((n,)),
            dma((n,)),
            dma((n,)),
            dma((K,)),
            dma((K,)),
            dma((K, chips)),
            dma((K, chips)),
        ],
        compiler_params=pltpu.CompilerParams(
            collective_id=0, has_side_effects=True, vmem_limit_bytes=56 * 1024 * 1024
        ),
    )(field_t, cot_t, mix_t, taps, offs, wids, cyc_f, cyc_b)
    output = jnp.swapaxes(out_t, 0, 1)
    field_grad = jnp.swapaxes(fgrad_t, 0, 1)
    mixing_grad = jnp.swapaxes(mgrad_t, 0, 1)
    if not direct:
        mixing_grad = lax.psum_scatter(mixing_grad, "lon", scatter_dimension=0, tiled=True)
    return (output, field_grad, mixing_grad)


def solution(mesh):
    in_specs = (P("grp", "lon", None), P("grp", "lon", None), P(), P(), P(), P(), P())
    out_specs = (P("grp", "lon", None), P("grp", "lon", None), P("lon", "grp", None))
    return jax.shard_map(
        functools.partial(body, mesh.shape["lon"]),
        mesh=mesh,
        in_specs=in_specs,
        out_specs=out_specs,
        check_vma=False,
    )
```

```python
import functools

import jax
import jax.numpy as jnp
from jax import lax
from jax.experimental import pallas as pl
from jax.experimental.pallas import tpu as pltpu
from jax.sharding import PartitionSpec as P

BAND = 8
R = 2
TAPS = 2 * R + 1
K = 3
POLAR = 6
PB = 8
MESH = pl.DeviceIdType.MESH
F32 = jnp.float32
BF16 = jnp.bfloat16


def kernel_body(
    n,
    direct,
    scale,
    field,
    cot_hbm,
    mix_hbm,
    taps,
    offs,
    wids,
    cyc,
    out,
    fgrad,
    mgrad,
    xt,
    cot,
    mix,
    pieces,
    fwd,
    bwd,
    conv,
    polar,
    mg,
    cg,
    ms,
    zbuf,
    sbuf,
    part,
    partb,
    r1,
    s1,
    ry,
    s2,
    r2,
    in_sem,
    h_send,
    h_recv,
    g_send,
    g_recv,
    z_send,
    z_recv,
    s_send,
    s_recv,
    a_send,
    a_recv,
    c_send,
    c_recv,
    b_send,
    b_recv,
):
    cols = field.shape[0]
    lat = field.shape[1]
    ch = field.shape[2]
    me = lax.axis_index("lon")
    right, left = lax.rem(me + 1, n), lax.rem(me + n - 1, n)

    barrier = pltpu.get_barrier_semaphore()

    def greet(d, carry):
        pl.semaphore_signal(
            barrier, inc=1, device_id={"lon": lax.rem(me + d, n)}, device_id_type=MESH
        )
        return carry

    lax.fori_loop(1, n, greet, 0)

    load_field = pltpu.make_async_copy(field, xt.at[pl.ds(R, cols)], in_sem.at[0])
    load_mix = pltpu.make_async_copy(mix_hbm, mix, in_sem.at[1])
    load_cot = pltpu.make_async_copy(cot_hbm, cot, in_sem.at[2])
    load_field.start()
    load_mix.start()
    load_cot.start()

    def loop(lo, hi, fn):
        def step(i, carry):
            fn(i)
            return carry

        lax.fori_loop(lo, hi, step, 0)

    def remote(src, dst, send, recv, peer):
        return pltpu.make_async_remote_copy(
            src_ref=src,
            dst_ref=dst,
            send_sem=send,
            recv_sem=recv,
            device_id={"lon": peer},
            device_id_type=MESH,
        )

    quads = n // 4
    quad = me // 4
    spot = lax.rem(me, 4)

    def near(buf, send, recv):
        def copy(d):
            peer = quad * 4 + lax.rem(spot + d, 4)
            return remote(buf.at[0], buf.at[d], send.at[d], recv.at[d], peer)

        return copy

    def far(buf, send, recv):
        def copy(d):
            peer = lax.rem(quad + d, quads) * 4 + spot
            return remote(
                buf.at[4], buf.at[4 + d], send.at[4 + d], recv.at[4 + d], peer
            )

        return copy

    def start_all(copy, count):
        loop(1, count, lambda d: copy(d).start())

    def wait_all(copy, count):
        loop(1, count, lambda d: copy(d).wait())

    def turn(buf, send, recv):
        wait_all(near(buf, send, recv), 4)
        buf[4] = jnp.sum(buf[0:4], axis=0)
        start_all(far(buf, send, recv), quads)

    pl.semaphore_wait(barrier, n - 1)
    halo_l = remote(
        field.at[pl.ds(0, R)], xt.at[pl.ds(R + cols, R)], h_send.at[0], h_recv.at[0], left
    )
    halo_r = remote(
        field.at[pl.ds(cols - R, R)], xt.at[pl.ds(0, R)], h_send.at[1], h_recv.at[1], right
    )
    halo_l.start()
    halo_r.start()
    load_field.wait()
    zbuf[0] = jnp.sum(xt[R : R + cols, 0:16, :].astype(F32), axis=0)[0:PB]
    start_all(near(zbuf, z_send, z_recv), 4)

    wide = 2 * K * lat
    rel = lax.broadcasted_iota(jnp.int32, (lat, wide), 0) - jnp.concatenate(
        [offs[...]] * (2 * K), axis=1
    )
    used = rel < jnp.concatenate([wids[...]] * (2 * K), axis=1)
    blank = jnp.zeros((BAND, lat), F32)
    for t in range(TAPS + 1):
        first = [taps[t, k].astype(F32) if t < TAPS else blank for k in range(K)]
        second = [taps[t - 1, k].astype(F32) if t > 0 else blank for k in range(K)]
        rows_bk = jnp.concatenate(first + second, axis=1)
        acc = jnp.zeros((lat, wide), F32)
        for b in range(BAND):
            acc = jnp.where((rel == b) & used, rows_bk[b : b + 1, :], acc)
        pieces[t * lat : (t + 1) * lat, :] = acc
    fwd[...] = pieces[...].T.astype(BF16)
    for a in range(4):
        for p in range(4):
            t = 2 * R - 2 * p + a
            if 0 <= t <= TAPS:
                block = pieces[t * lat : (t + 1) * lat, :].astype(BF16)
            else:
                block = jnp.zeros((lat, wide), BF16)
            bwd[a * lat : (a + 1) * lat, p * wide : (p + 1) * wide] = block

    turn(zbuf, z_send, z_recv)

    def conv_pair(p):
        source = xt[pl.ds(2 * p, TAPS + 1)].reshape((TAPS + 1) * lat, ch)
        c = jnp.dot(fwd[...], source, preferred_element_type=F32)
        c = c.reshape(2, K, lat, ch)
        polar[pl.ds(2 * p, 2)] = c[:, :, 0:16]
        conv[pl.ds(2 * p, 2)] = c.astype(BF16)

    pairs = cols // 2
    loop(1, pairs - 1, conv_pair)
    halo_l.wait()
    halo_r.wait()
    loop(0, 2, lambda i: conv_pair(i * (pairs - 1)))

    wait_all(far(zbuf, z_send, z_recv), quads)
    zonal = jnp.sum(zbuf[4:], axis=0) * scale
    lines = []
    for k in range(K):
        for i in range(POLAR):
            line = cyc[i, k, 0] * zonal[0:1]
            for p in range(1, PB):
                line = line + cyc[i, k, p] * zonal[p : p + 1]
            lines.append(line)
        lines.append(jnp.zeros((16 - POLAR, ch), F32))
    term = jnp.concatenate(lines, axis=0).reshape(1, K, 16, ch)
    load_mix.wait()
    load_cot.wait()
    ms[...] = jnp.zeros_like(ms)

    def mix_group(g):
        at = pl.ds(4 * g, 4)
        conv[at, :, 0:16] = (polar[at] + term).astype(BF16)
        mixed = jnp.dot(
            conv[at, 0].reshape(4 * lat, ch), mix[0], preferred_element_type=F32
        )
        for k in range(1, K):
            mixed = mixed + jnp.dot(
                conv[at, k].reshape(4 * lat, ch), mix[k], preferred_element_type=F32
            )
        sig = jax.nn.sigmoid(mixed)
        out[at] = (mixed * sig).astype(BF16).reshape(4, lat, ch)
        ct = cot[at].reshape(4 * lat, ch).astype(F32)
        grad = (ct * (sig * (1.0 + mixed * (1.0 - sig)))).astype(BF16).reshape(4, lat, ch)
        mg[pl.ds(R + 4 * g, 4)] = grad
        ms[...] += jnp.sum(grad[:, 0:16].astype(F32), axis=0)

    groups = cols // 4
    loop(0, 2, lambda i: mix_group(i * (groups - 1)))
    grad_l = remote(
        mg.at[pl.ds(R, R)], mg.at[pl.ds(R + cols, R)], g_send.at[0], g_recv.at[0], left
    )
    grad_r = remote(
        mg.at[pl.ds(cols, R)], mg.at[pl.ds(0, R)], g_send.at[1], g_recv.at[1], right
    )
    grad_l.start()
    grad_r.start()
    loop(1, groups - 1, mix_group)
    sbuf[0] = ms[0:PB]
    start_all(near(sbuf, s_send, s_recv), 4)

    half = ch // 2
    if direct:
        rows = ch // n
        core = lax.rem(me, 2)
        side = lax.rem(me // 2, 2)
        per = half // (4 * rows)

        def core_copy(k):
            return remote(
                partb.at[k, 1 - core],
                r1.at[k],
                a_send.at[k],
                a_recv.at[k],
                quad * 4 + side * 2 + (1 - core),
            )

        def side_copy(k):
            return remote(
                s1.at[k],
                ry.at[k],
                c_send.at[k],
                c_recv.at[k],
                quad * 4 + (1 - side) * 2 + core,
            )

        def quad_copy(k, d):
            return remote(
                s2.at[k, d],
                r2.at[k, d],
                b_send.at[k, d],
                b_recv.at[k, d],
                lax.rem(quad + d, quads) * 4 + spot,
            )

        def pass_side(k):
            core_copy(k).wait()

            def step(z):
                s1[k, z] = (
                    part[k, core, 1 - side, z] + r1[k, 1 - side, z].astype(F32)
                ).astype(BF16)

            loop(0, quads, step)
            side_copy(k).start()

        def own(k, z):
            return (
                part[k, core, side, z]
                + r1[k, side, z].astype(F32)
                + ry[k, z].astype(F32)
            )

        def pass_quads(k):
            side_copy(k).wait()

            def step(d):
                s2[k, d] = own(k, lax.rem(quad + d, quads)).astype(BF16)
                quad_copy(k, d).start()

            loop(1, quads, step)

    for k in range(K):

        def product(h):
            lanes = pl.ds(pl.multiple_of(h * half, half), half)
            res = lax.dot_general(
                conv[:, k, :, lanes].reshape(cols * lat, half),
                mg[R : R + cols].reshape(cols * lat, ch),
                (((0,), (0,)), ((), ())),
                preferred_element_type=F32,
            )
            if not direct:
                mgrad[k, lanes, :] = res
                return
            res = res.reshape(per, 2, 2, rows, ch)
            resb = res.astype(BF16)
            for y in range(2):
                for c in range(2):
                    part[k, c, y, pl.ds(h * per, per)] = res[:, y, c]
                    partb[k, c, y, pl.ds(h * per, per)] = resb[:, y, c]

        loop(0, 2, product)
        if direct:
            core_copy(k).start()
            if k > 0:
                pass_side(k - 1)
        if k == 0:
            turn(sbuf, s_send, s_recv)
    if direct:
        pass_quads(0)
        pass_side(K - 1)

    def spread_grad(g):
        at = pl.ds(4 * g, 4)
        source = mg[at].reshape(4 * lat, ch)
        for k in range(K):
            res = lax.dot_general(
                source, mix[k], (((1,), (1,)), ((), ())), preferred_element_type=F32
            )
            cg[at, k] = res.astype(BF16).reshape(4, lat, ch)

    loop(1, groups, spread_grad)
    grad_l.wait()
    grad_r.wait()
    loop(0, 2, lambda i: spread_grad(i * groups))
    if direct:
        pass_quads(1)

    wait_all(far(sbuf, s_send, s_recv), quads)
    total = jnp.sum(sbuf[4:], axis=0)
    high = total.astype(BF16)
    low = (total - high.astype(F32)).astype(BF16)
    both = jnp.concatenate([high.astype(F32), low.astype(F32)], axis=0).astype(BF16)
    lines = [jnp.zeros((1, ch), F32)] * PB
    for k in range(K):
        res = lax.dot_general(
            both, mix[k], (((1,), (1,)), ((), ())), preferred_element_type=F32
        )
        res = res[0:PB] + res[PB : 2 * PB]
        for i in range(POLAR):
            for q in range(PB):
                lines[q] = lines[q] + (cyc[i, k, q] * scale) * res[i : i + 1]
    lines.append(jnp.zeros((16 - PB, ch), F32))
    zgrad = jnp.concatenate(lines, axis=0)[None]

    def field_group(g):
        at = pl.ds(4 * g, 4)
        source = cg[pl.ds(4 * g, 8)].reshape(8 * K * lat, ch)
        res = jnp.dot(bwd[...], source, preferred_element_type=F32).reshape(4, lat, ch)
        fgrad[at] = res.astype(BF16)
        fgrad[at, 0:16] = (res[:, 0:16] + zgrad).astype(BF16)

    loop(0, groups, field_group)

    if direct:
        pass_quads(K - 1)
        for k in range(K):
            acc = own(k, quad)
            for d in range(1, quads):
                quad_copy(k, d).wait()
                acc = acc + r2[k, d].astype(F32)
            mgrad[k] = acc


def body(n, field, cotangent, offsets, widths, kernel, cycle, mixing):
    lat, cols, ch = field.shape
    scale = float(cols * n) ** (-0.5)
    rows = ch // n
    direct = rows % 16 == 0 and ch % (8 * rows) == 0
    field_t = jnp.swapaxes(field, 0, 1)
    cot_t = jnp.swapaxes(cotangent, 0, 1)
    mix_t = jnp.swapaxes(mixing, 0, 1)
    taps = jnp.transpose(kernel, (2, 3, 1, 0))
    offs = offsets.reshape(1, lat)
    wids = widths.reshape(1, lat)
    cyc = jnp.swapaxes(cycle, 1, 2)

    wide = 2 * K * lat
    dma = pltpu.SemaphoreType.DMA
    quads = n // 4 if direct else 1
    brows = rows if direct else 16
    vmem = pl.BlockSpec(memory_space=pltpu.VMEM)
    hbm = pl.BlockSpec(memory_space=pl.ANY)
    out_t, fgrad_t, mgrad_t = pl.pallas_call(
        functools.partial(kernel_body, n, direct, scale),
        out_shape=[
            jax.ShapeDtypeStruct((cols, lat, ch), BF16),
            jax.ShapeDtypeStruct((cols, lat, ch), BF16),
            jax.ShapeDtypeStruct((K, rows if direct else ch, ch), F32),
        ],
        in_specs=[hbm] * 3 + [vmem] * 3 + [pl.BlockSpec(memory_space=pltpu.SMEM)],
        out_specs=[vmem] * 3,
        scratch_shapes=[
            pltpu.VMEM((cols + 2 * R, lat, ch), BF16),
            pltpu.VMEM((cols, lat, ch), BF16),
            pltpu.VMEM((K, ch, ch), BF16),
            pltpu.VMEM(((TAPS + 1) * lat, wide), F32),
            pltpu.VMEM((wide, (TAPS + 1) * lat), BF16),
            pltpu.VMEM((4 * lat, 4 * wide), BF16),
            pltpu.VMEM((cols, K, lat, ch), BF16),
            pltpu.VMEM((cols, K, 16, ch), F32),
            pltpu.VMEM((cols + 2 * R, lat, ch), BF16),
            pltpu.VMEM((cols + 2 * R, K, lat, ch), BF16),
            pltpu.VMEM((16, ch), F32),
            pltpu.VMEM((4 + n // 4, PB, ch), F32),
            pltpu.VMEM((4 + n // 4, PB, ch), F32),
            pltpu.VMEM((K, 2, 2, quads, brows, ch), F32),
            pltpu.VMEM((K, 2, 2, quads, brows, ch), BF16),
            pltpu.VMEM((K, 2, quads, brows, ch), BF16),
            pltpu.VMEM((K, quads, brows, ch), BF16),
            pltpu.VMEM((K, quads, brows, ch), BF16),
            pltpu.VMEM((K, quads, brows, ch), BF16),
            pltpu.VMEM((K, quads, brows, ch), BF16),
            dma((3,)),
            dma((2,)),
            dma((2,)),
            dma((2,)),
            dma((2,)),
            dma((4 + n // 4,)),
            dma((4 + n // 4,)),
            dma((4 + n // 4,)),
            dma((4 + n // 4,)),
            dma((K,)),
            dma((K,)),
            dma((K,)),
            dma((K,)),
            dma((K, quads)),
            dma((K, quads)),
        ],
        compiler_params=pltpu.CompilerParams(
            collective_id=0, has_side_effects=True, vmem_limit_bytes=56 * 1024 * 1024
        ),
    )(field_t, cot_t, mix_t, taps, offs, wids, cyc)
    output = jnp.swapaxes(out_t, 0, 1)
    field_grad = jnp.swapaxes(fgrad_t, 0, 1)
    mixing_grad = jnp.swapaxes(mgrad_t, 0, 1)
    if not direct:
        mixing_grad = lax.psum_scatter(mixing_grad, "lon", scatter_dimension=0, tiled=True)
    return (output, field_grad, mixing_grad)


def solution(mesh):
    in_specs = (P("grp", "lon", None), P("grp", "lon", None), P(), P(), P(), P(), P())
    out_specs = (P("grp", "lon", None), P("grp", "lon", None), P("lon", "grp", None))
    return jax.shard_map(
        functools.partial(body, mesh.shape["lon"]),
        mesh=mesh,
        in_specs=in_specs,
        out_specs=out_specs,
        check_vma=False,
    )
```

```python
import functools

import jax
import jax.numpy as jnp
from jax import lax
from jax.experimental import pallas as pl
from jax.experimental.pallas import tpu as pltpu
from jax.sharding import PartitionSpec as P

BAND = 8
R = 2
TAPS = 2 * R + 1
K = 3
POLAR = 6
PB = 8
MESH = pl.DeviceIdType.MESH
F32 = jnp.float32
BF16 = jnp.bfloat16


def kernel_body(
    n,
    direct,
    scale,
    field,
    cot_hbm,
    mix_hbm,
    taps,
    offs,
    wids,
    cyc,
    out,
    fgrad,
    mgrad,
    xt,
    cot,
    mix,
    pieces,
    fwd,
    bwd,
    conv,
    polar,
    mg,
    cg,
    ms,
    zbuf,
    sbuf,
    part,
    partb,
    r1,
    s1,
    ry,
    s2,
    r2,
    in_sem,
    h_send,
    h_recv,
    g_send,
    g_recv,
    z_send,
    z_recv,
    s_send,
    s_recv,
    a_send,
    a_recv,
    c_send,
    c_recv,
    b_send,
    b_recv,
):
    cols = field.shape[0]
    lat = field.shape[1]
    ch = field.shape[2]
    me = lax.axis_index("lon")
    right, left = lax.rem(me + 1, n), lax.rem(me + n - 1, n)

    barrier = pltpu.get_barrier_semaphore()

    def greet(d, carry):
        pl.semaphore_signal(
            barrier, inc=1, device_id={"lon": lax.rem(me + d, n)}, device_id_type=MESH
        )
        return carry

    lax.fori_loop(1, n, greet, 0)

    load_field = pltpu.make_async_copy(field, xt.at[pl.ds(R, cols)], in_sem.at[0])
    load_mix = pltpu.make_async_copy(mix_hbm, mix, in_sem.at[1])
    load_cot = pltpu.make_async_copy(cot_hbm, cot, in_sem.at[2])
    load_field.start()
    load_mix.start()
    load_cot.start()

    def loop(lo, hi, fn):
        def step(i, carry):
            fn(i)
            return carry

        lax.fori_loop(lo, hi, step, 0)

    def remote(src, dst, send, recv, peer):
        return pltpu.make_async_remote_copy(
            src_ref=src,
            dst_ref=dst,
            send_sem=send,
            recv_sem=recv,
            device_id={"lon": peer},
            device_id_type=MESH,
        )

    quads = n // 4
    quad = me // 4
    spot = lax.rem(me, 4)

    def near(buf, send, recv):
        def copy(d):
            peer = quad * 4 + lax.rem(spot + d, 4)
            return remote(buf.at[0], buf.at[d], send.at[d], recv.at[d], peer)

        return copy

    def far(buf, send, recv):
        def copy(d):
            peer = lax.rem(quad + d, quads) * 4 + spot
            return remote(
                buf.at[4], buf.at[4 + d], send.at[4 + d], recv.at[4 + d], peer
            )

        return copy

    def start_all(copy, count):
        loop(1, count, lambda d: copy(d).start())

    def wait_all(copy, count):
        loop(1, count, lambda d: copy(d).wait())

    def turn(buf, send, recv):
        wait_all(near(buf, send, recv), 4)
        buf[4] = jnp.sum(buf[0:4], axis=0)
        start_all(far(buf, send, recv), quads)

    pl.semaphore_wait(barrier, n - 1)
    halo_l = remote(
        field.at[pl.ds(0, R)], xt.at[pl.ds(R + cols, R)], h_send.at[0], h_recv.at[0], left
    )
    halo_r = remote(
        field.at[pl.ds(cols - R, R)], xt.at[pl.ds(0, R)], h_send.at[1], h_recv.at[1], right
    )
    halo_l.start()
    halo_r.start()
    load_field.wait()
    zbuf[0] = jnp.sum(xt[R : R + cols, 0:16, :].astype(F32), axis=0)[0:PB]
    start_all(near(zbuf, z_send, z_recv), 4)

    wide = 2 * K * lat
    rel = lax.broadcasted_iota(jnp.int32, (lat, wide), 0) - jnp.concatenate(
        [offs[...]] * (2 * K), axis=1
    )
    used = rel < jnp.concatenate([wids[...]] * (2 * K), axis=1)
    blank = jnp.zeros((BAND, lat), F32)
    for t in range(TAPS + 1):
        first = [taps[t, k].astype(F32) if t < TAPS else blank for k in range(K)]
        second = [taps[t - 1, k].astype(F32) if t > 0 else blank for k in range(K)]
        rows_bk = jnp.concatenate(first + second, axis=1)
        acc = jnp.zeros((lat, wide), F32)
        for b in range(BAND):
            acc = jnp.where((rel == b) & used, rows_bk[b : b + 1, :], acc)
        pieces[t * lat : (t + 1) * lat, :] = acc
    fwd[...] = pieces[...].T.astype(BF16)
    for a in range(4):
        for p in range(4):
            t = 2 * R - 2 * p + a
            if 0 <= t <= TAPS:
                block = pieces[t * lat : (t + 1) * lat, :].astype(BF16)
            else:
                block = jnp.zeros((lat, wide), BF16)
            bwd[a * lat : (a + 1) * lat, p * wide : (p + 1) * wide] = block

    turn(zbuf, z_send, z_recv)

    def conv_pair(p):
        source = xt[pl.ds(2 * p, TAPS + 1)].reshape((TAPS + 1) * lat, ch)
        c = jnp.dot(fwd[...], source, preferred_element_type=F32)
        c = c.reshape(2, K, lat, ch)
        polar[pl.ds(2 * p, 2)] = c[:, :, 0:16]
        conv[pl.ds(2 * p, 2)] = c.astype(BF16)

    pairs = cols // 2
    loop(1, pairs - 1, conv_pair)
    halo_l.wait()
    halo_r.wait()
    loop(0, 2, lambda i: conv_pair(i * (pairs - 1)))

    wait_all(far(zbuf, z_send, z_recv), quads)
    zonal = jnp.sum(zbuf[4:], axis=0) * scale
    lines = []
    for k in range(K):
        for i in range(POLAR):
            line = cyc[i, k, 0] * zonal[0:1]
            for p in range(1, PB):
                line = line + cyc[i, k, p] * zonal[p : p + 1]
            lines.append(line)
        lines.append(jnp.zeros((16 - POLAR, ch), F32))
    term = jnp.concatenate(lines, axis=0).reshape(1, K, 16, ch)
    load_mix.wait()
    load_cot.wait()
    ms[...] = jnp.zeros_like(ms)

    def mix_group(g):
        at = pl.ds(4 * g, 4)
        conv[at, :, 0:16] = (polar[at] + term).astype(BF16)
        mixed = jnp.dot(
            conv[at, 0].reshape(4 * lat, ch), mix[0], preferred_element_type=F32
        )
        for k in range(1, K):
            mixed = mixed + jnp.dot(
                conv[at, k].reshape(4 * lat, ch), mix[k], preferred_element_type=F32
            )
        sig = jax.nn.sigmoid(mixed)
        out[at] = (mixed * sig).astype(BF16).reshape(4, lat, ch)
        ct = cot[at].reshape(4 * lat, ch).astype(F32)
        grad = (ct * (sig * (1.0 + mixed * (1.0 - sig)))).astype(BF16).reshape(4, lat, ch)
        mg[pl.ds(R + 4 * g, 4)] = grad
        ms[...] += jnp.sum(grad[:, 0:16].astype(F32), axis=0)

    groups = cols // 4
    loop(0, 2, lambda i: mix_group(i * (groups - 1)))
    grad_l = remote(
        mg.at[pl.ds(R, R)], mg.at[pl.ds(R + cols, R)], g_send.at[0], g_recv.at[0], left
    )
    grad_r = remote(
        mg.at[pl.ds(cols, R)], mg.at[pl.ds(0, R)], g_send.at[1], g_recv.at[1], right
    )
    grad_l.start()
    grad_r.start()
    loop(1, groups - 1, mix_group)
    sbuf[0] = ms[0:PB]
    start_all(near(sbuf, s_send, s_recv), 4)

    half = ch // 2
    if direct:
        rows = ch // n
        core = lax.rem(me, 2)
        side = lax.rem(me // 2, 2)
        per = half // (4 * rows)

        def core_copy(k):
            return remote(
                partb.at[k, 1 - core],
                r1.at[k],
                a_send.at[k],
                a_recv.at[k],
                quad * 4 + side * 2 + (1 - core),
            )

        def side_copy(k):
            return remote(
                s1.at[k],
                ry.at[k],
                c_send.at[k],
                c_recv.at[k],
                quad * 4 + (1 - side) * 2 + core,
            )

        def quad_copy(k, d):
            return remote(
                s2.at[k, d],
                r2.at[k, d],
                b_send.at[k, d],
                b_recv.at[k, d],
                lax.rem(quad + d, quads) * 4 + spot,
            )

        def pass_side(k):
            core_copy(k).wait()

            def step(z):
                s1[k, z] = (
                    part[k, core, 1 - side, z] + r1[k, 1 - side, z].astype(F32)
                ).astype(BF16)

            loop(0, quads, step)
            side_copy(k).start()

        def own(k, z):
            return (
                part[k, core, side, z]
                + r1[k, side, z].astype(F32)
                + ry[k, z].astype(F32)
            )

        def pass_quads(k):
            side_copy(k).wait()

            def step(d):
                s2[k, d] = own(k, lax.rem(quad + d, quads)).astype(BF16)
                quad_copy(k, d).start()

            loop(1, quads, step)

    for k in range(K):

        def product(h):
            lanes = pl.ds(pl.multiple_of(h * half, half), half)
            res = lax.dot_general(
                conv[:, k, :, lanes].reshape(cols * lat, half),
                mg[R : R + cols].reshape(cols * lat, ch),
                (((0,), (0,)), ((), ())),
                preferred_element_type=F32,
            )
            if not direct:
                mgrad[k, lanes, :] = res
                return
            res = res.reshape(per, 2, 2, rows, ch)
            resb = res.astype(BF16)
            for y in range(2):
                for c in range(2):
                    part[k, c, y, pl.ds(h * per, per)] = res[:, y, c]
                    partb[k, c, y, pl.ds(h * per, per)] = resb[:, y, c]

        loop(0, 2, product)
        if direct:
            core_copy(k).start()
            if k > 0:
                pass_side(k - 1)
        if k == 0:
            turn(sbuf, s_send, s_recv)
    if direct:
        pass_quads(0)
        pass_side(K - 1)

    def spread_grad(g):
        at = pl.ds(4 * g, 4)
        source = mg[at].reshape(4 * lat, ch)
        for k in range(K):
            res = lax.dot_general(
                source, mix[k], (((1,), (1,)), ((), ())), preferred_element_type=F32
            )
            cg[at, k] = res.astype(BF16).reshape(4, lat, ch)

    loop(1, groups, spread_grad)
    grad_l.wait()
    grad_r.wait()
    loop(0, 2, lambda i: spread_grad(i * groups))
    if direct:
        pass_quads(1)

    wait_all(far(sbuf, s_send, s_recv), quads)
    total = jnp.sum(sbuf[4:], axis=0)
    high = total.astype(BF16)
    low = (total - high.astype(F32)).astype(BF16)
    both = jnp.concatenate([high.astype(F32), low.astype(F32)], axis=0).astype(BF16)
    lines = [jnp.zeros((1, ch), F32)] * PB
    for k in range(K):
        res = lax.dot_general(
            both, mix[k], (((1,), (1,)), ((), ())), preferred_element_type=F32
        )
        res = res[0:PB] + res[PB : 2 * PB]
        for i in range(POLAR):
            for q in range(PB):
                lines[q] = lines[q] + (cyc[i, k, q] * scale) * res[i : i + 1]
    lines.append(jnp.zeros((16 - PB, ch), F32))
    zgrad = jnp.concatenate(lines, axis=0)[None]

    def field_group(g):
        at = pl.ds(4 * g, 4)
        source = cg[pl.ds(4 * g, 8)].reshape(8 * K * lat, ch)
        res = jnp.dot(bwd[...], source, preferred_element_type=F32).reshape(4, lat, ch)
        fgrad[at] = res.astype(BF16)
        fgrad[at, 0:16] = (res[:, 0:16] + zgrad).astype(BF16)

    loop(0, groups, field_group)

    if direct:
        pass_quads(K - 1)
        for k in range(K):
            acc = own(k, quad)
            for d in range(1, quads):
                quad_copy(k, d).wait()
                acc = acc + r2[k, d].astype(F32)
            mgrad[k] = acc


def body(n, field, cotangent, offsets, widths, kernel, cycle, mixing):
    lat, cols, ch = field.shape
    scale = float(cols * n) ** (-0.5)
    rows = ch // n
    direct = rows % 16 == 0 and ch % (8 * rows) == 0
    field_t = jnp.swapaxes(field, 0, 1)
    cot_t = jnp.swapaxes(cotangent, 0, 1)
    mix_t = jnp.swapaxes(mixing, 0, 1)
    taps = jnp.transpose(kernel, (2, 3, 1, 0))
    offs = offsets.reshape(1, lat)
    wids = widths.reshape(1, lat)
    cyc = jnp.swapaxes(cycle, 1, 2)

    wide = 2 * K * lat
    dma = pltpu.SemaphoreType.DMA
    quads = n // 4 if direct else 1
    brows = rows if direct else 16
    vmem = pl.BlockSpec(memory_space=pltpu.VMEM)
    hbm = pl.BlockSpec(memory_space=pl.ANY)
    out_t, fgrad_t, mgrad_t = pl.pallas_call(
        functools.partial(kernel_body, n, direct, scale),
        out_shape=[
            jax.ShapeDtypeStruct((cols, lat, ch), BF16),
            jax.ShapeDtypeStruct((cols, lat, ch), BF16),
            jax.ShapeDtypeStruct((K, rows if direct else ch, ch), F32),
        ],
        in_specs=[hbm] * 3 + [vmem] * 3 + [pl.BlockSpec(memory_space=pltpu.SMEM)],
        out_specs=[vmem] * 3,
        scratch_shapes=[
            pltpu.VMEM((cols + 2 * R, lat, ch), BF16),
            pltpu.VMEM((cols, lat, ch), BF16),
            pltpu.VMEM((K, ch, ch), BF16),
            pltpu.VMEM(((TAPS + 1) * lat, wide), F32),
            pltpu.VMEM((wide, (TAPS + 1) * lat), BF16),
            pltpu.VMEM((4 * lat, 4 * wide), BF16),
            pltpu.VMEM((cols, K, lat, ch), BF16),
            pltpu.VMEM((cols, K, 16, ch), F32),
            pltpu.VMEM((cols + 2 * R, lat, ch), BF16),
            pltpu.VMEM((cols + 2 * R, K, lat, ch), BF16),
            pltpu.VMEM((16, ch), F32),
            pltpu.VMEM((4 + n // 4, PB, ch), F32),
            pltpu.VMEM((4 + n // 4, PB, ch), F32),
            pltpu.VMEM((K, 2, 2, quads, brows, ch), F32),
            pltpu.VMEM((K, 2, 2, quads, brows, ch), BF16),
            pltpu.VMEM((K, 2, quads, brows, ch), BF16),
            pltpu.VMEM((K, quads, brows, ch), BF16),
            pltpu.VMEM((K, quads, brows, ch), BF16),
            pltpu.VMEM((K, quads, brows, ch), BF16),
            pltpu.VMEM((K, quads, brows, ch), BF16),
            dma((3,)),
            dma((2,)),
            dma((2,)),
            dma((2,)),
            dma((2,)),
            dma((4 + n // 4,)),
            dma((4 + n // 4,)),
            dma((4 + n // 4,)),
            dma((4 + n // 4,)),
            dma((K,)),
            dma((K,)),
            dma((K,)),
            dma((K,)),
            dma((K, quads)),
            dma((K, quads)),
        ],
        compiler_params=pltpu.CompilerParams(
            collective_id=0, has_side_effects=True, vmem_limit_bytes=36 * 1024 * 1024
        ),
    )(field_t, cot_t, mix_t, taps, offs, wids, cyc)
    output = jnp.swapaxes(out_t, 0, 1)
    field_grad = jnp.swapaxes(fgrad_t, 0, 1)
    mixing_grad = jnp.swapaxes(mgrad_t, 0, 1)
    if not direct:
        mixing_grad = lax.psum_scatter(mixing_grad, "lon", scatter_dimension=0, tiled=True)
    return (output, field_grad, mixing_grad)


def solution(mesh):
    in_specs = (P("grp", "lon", None), P("grp", "lon", None), P(), P(), P(), P(), P())
    out_specs = (P("grp", "lon", None), P("grp", "lon", None), P("lon", "grp", None))
    return jax.shard_map(
        functools.partial(body, mesh.shape["lon"]),
        mesh=mesh,
        in_specs=in_specs,
        out_specs=out_specs,
        check_vma=False,
    )
```

```python
import functools

import jax
import jax.numpy as jnp
from jax import lax
from jax.experimental import pallas as pl
from jax.experimental.pallas import tpu as pltpu
from jax.sharding import PartitionSpec as P

BAND = 8
R = 2
TAPS = 2 * R + 1
K = 3
POLAR = 6
PB = 8
MESH = pl.DeviceIdType.MESH
F32 = jnp.float32
BF16 = jnp.bfloat16


def kernel_body(
    n,
    direct,
    scale,
    field,
    cot_hbm,
    mix_hbm,
    taps,
    offs,
    wids,
    cyc,
    out,
    fgrad,
    mgrad,
    xt,
    cot,
    mix,
    pieces,
    fwd,
    bwd,
    conv,
    polar,
    mg,
    cg,
    ms,
    zbuf,
    sbuf,
    part,
    partb,
    r1,
    s1,
    ry,
    s2,
    r2,
    in_sem,
    h_send,
    h_recv,
    g_send,
    g_recv,
    z_send,
    z_recv,
    s_send,
    s_recv,
    a_send,
    a_recv,
    c_send,
    c_recv,
    b_send,
    b_recv,
):
    cols = field.shape[0]
    lat = field.shape[1]
    ch = field.shape[2]
    me = lax.axis_index("lon")
    right, left = lax.rem(me + 1, n), lax.rem(me + n - 1, n)

    barrier = pltpu.get_barrier_semaphore()

    def greet(d, carry):
        pl.semaphore_signal(
            barrier, inc=1, device_id={"lon": lax.rem(me + d, n)}, device_id_type=MESH
        )
        return carry

    lax.fori_loop(1, n, greet, 0)

    load_field = pltpu.make_async_copy(field, xt.at[pl.ds(R, cols)], in_sem.at[0])
    load_mix = pltpu.make_async_copy(mix_hbm, mix, in_sem.at[1])
    load_cot = pltpu.make_async_copy(cot_hbm, cot, in_sem.at[2])
    load_field.start()
    load_mix.start()
    load_cot.start()

    def loop(lo, hi, fn):
        def step(i, carry):
            fn(i)
            return carry

        lax.fori_loop(lo, hi, step, 0)

    def remote(src, dst, send, recv, peer):
        return pltpu.make_async_remote_copy(
            src_ref=src,
            dst_ref=dst,
            send_sem=send,
            recv_sem=recv,
            device_id={"lon": peer},
            device_id_type=MESH,
        )

    quads = n // 4
    quad = me // 4
    spot = lax.rem(me, 4)

    def near(buf, send, recv):
        def copy(d):
            peer = quad * 4 + lax.rem(spot + d, 4)
            return remote(buf.at[0], buf.at[d], send.at[d], recv.at[d], peer)

        return copy

    def far(buf, send, recv):
        def copy(d):
            peer = lax.rem(quad + d, quads) * 4 + spot
            return remote(
                buf.at[4], buf.at[4 + d], send.at[4 + d], recv.at[4 + d], peer
            )

        return copy

    def start_all(copy, count):
        loop(1, count, lambda d: copy(d).start())

    def wait_all(copy, count):
        loop(1, count, lambda d: copy(d).wait())

    def turn(buf, send, recv):
        wait_all(near(buf, send, recv), 4)
        buf[4] = jnp.sum(buf[0:4], axis=0)
        start_all(far(buf, send, recv), quads)

    pl.semaphore_wait(barrier, n - 1)
    halo_l = remote(
        field.at[pl.ds(0, R)], xt.at[pl.ds(R + cols, R)], h_send.at[0], h_recv.at[0], left
    )
    halo_r = remote(
        field.at[pl.ds(cols - R, R)], xt.at[pl.ds(0, R)], h_send.at[1], h_recv.at[1], right
    )
    halo_l.start()
    halo_r.start()
    load_field.wait()
    zbuf[0] = jnp.sum(xt[R : R + cols, 0:16, :].astype(F32), axis=0)[0:PB]
    start_all(near(zbuf, z_send, z_recv), 4)

    wide = 2 * K * lat
    rel = lax.broadcasted_iota(jnp.int32, (lat, wide), 0) - jnp.concatenate(
        [offs[...]] * (2 * K), axis=1
    )
    used = rel < jnp.concatenate([wids[...]] * (2 * K), axis=1)
    blank = jnp.zeros((BAND, lat), F32)
    for t in range(TAPS + 1):
        first = [taps[t, k].astype(F32) if t < TAPS else blank for k in range(K)]
        second = [taps[t - 1, k].astype(F32) if t > 0 else blank for k in range(K)]
        rows_bk = jnp.concatenate(first + second, axis=1)
        acc = jnp.zeros((lat, wide), F32)
        for b in range(BAND):
            acc = jnp.where((rel == b) & used, rows_bk[b : b + 1, :], acc)
        pieces[t * lat : (t + 1) * lat, :] = acc
    fwd[...] = pieces[...].T.astype(BF16)
    for a in range(4):
        for p in range(4):
            t = 2 * R - 2 * p + a
            if 0 <= t <= TAPS:
                block = pieces[t * lat : (t + 1) * lat, :].astype(BF16)
            else:
                block = jnp.zeros((lat, wide), BF16)
            bwd[a * lat : (a + 1) * lat, p * wide : (p + 1) * wide] = block

    turn(zbuf, z_send, z_recv)

    def conv_pair(p):
        source = xt[pl.ds(2 * p, TAPS + 1)].reshape((TAPS + 1) * lat, ch)
        c = jnp.dot(fwd[...], source, preferred_element_type=F32)
        c = c.reshape(2, K, lat, ch)
        polar[pl.ds(2 * p, 2)] = c[:, :, 0:16]
        conv[pl.ds(2 * p, 2)] = c.astype(BF16)

    pairs = cols // 2
    loop(1, pairs - 1, conv_pair)
    halo_l.wait()
    halo_r.wait()
    loop(0, 2, lambda i: conv_pair(i * (pairs - 1)))

    load_mix.wait()
    load_cot.wait()

    def mix_rows(first, count, lo, hi):
        at = pl.ds(first, count)
        size, shape = count * (hi - lo), (count, hi - lo, ch)
        mixed = jnp.dot(
            conv[at, 0, lo:hi].reshape(size, ch), mix[0], preferred_element_type=F32
        )
        for k in range(1, K):
            mixed = mixed + jnp.dot(
                conv[at, k, lo:hi].reshape(size, ch), mix[k], preferred_element_type=F32
            )
        sig = jax.nn.sigmoid(mixed)
        out[at, lo:hi] = (mixed * sig).astype(BF16).reshape(shape)
        ct = cot[at, lo:hi].reshape(size, ch).astype(F32)
        grad = (ct * (sig * (1.0 + mixed * (1.0 - sig)))).astype(BF16).reshape(shape)
        mg[pl.ds(R + first, count), lo:hi] = grad
        return grad

    groups = cols // 4

    def mix_group(g):
        mix_rows(4 * g, 4, 16, lat)

    loop(0, groups, mix_group)
    wait_all(far(zbuf, z_send, z_recv), quads)
    zonal = jnp.sum(zbuf[4:], axis=0) * scale
    lines = []
    for k in range(K):
        for i in range(POLAR):
            line = cyc[i, k, 0] * zonal[0:1]
            for p in range(1, PB):
                line = line + cyc[i, k, p] * zonal[p : p + 1]
            lines.append(line)
        lines.append(jnp.zeros((16 - POLAR, ch), F32))
    term = jnp.concatenate(lines, axis=0).reshape(1, K, 16, ch)
    conv[:, :, 0:16] = (polar[...] + term).astype(BF16)
    ms[...] = jnp.sum(mix_rows(0, cols, 0, 16).astype(F32), axis=0)
    grad_l = remote(
        mg.at[pl.ds(R, R)], mg.at[pl.ds(R + cols, R)], g_send.at[0], g_recv.at[0], left
    )
    grad_r = remote(
        mg.at[pl.ds(cols, R)], mg.at[pl.ds(0, R)], g_send.at[1], g_recv.at[1], right
    )
    grad_l.start()
    grad_r.start()
    sbuf[0] = ms[0:PB]
    start_all(near(sbuf, s_send, s_recv), 4)

    half = ch // 2
    if direct:
        rows = ch // n
        core = lax.rem(me, 2)
        side = lax.rem(me // 2, 2)
        per = half // (4 * rows)

        def core_copy(k):
            return remote(
                partb.at[k, 1 - core],
                r1.at[k],
                a_send.at[k],
                a_recv.at[k],
                quad * 4 + side * 2 + (1 - core),
            )

        def side_copy(k):
            return remote(
                s1.at[k],
                ry.at[k],
                c_send.at[k],
                c_recv.at[k],
                quad * 4 + (1 - side) * 2 + core,
            )

        def quad_copy(k, d):
            return remote(
                s2.at[k, d],
                r2.at[k, d],
                b_send.at[k, d],
                b_recv.at[k, d],
                lax.rem(quad + d, quads) * 4 + spot,
            )

        def pass_side(k):
            core_copy(k).wait()

            def step(z):
                s1[k, z] = (
                    part[k, core, 1 - side, z] + r1[k, 1 - side, z].astype(F32)
                ).astype(BF16)

            loop(0, quads, step)
            side_copy(k).start()

        def own(k, z):
            return (
                part[k, core, side, z]
                + r1[k, side, z].astype(F32)
                + ry[k, z].astype(F32)
            )

        def pass_quads(k):
            side_copy(k).wait()

            def step(d):
                s2[k, d] = own(k, lax.rem(quad + d, quads)).astype(BF16)
                quad_copy(k, d).start()

            loop(1, quads, step)

    for k in range(K):

        def product(h):
            lanes = pl.ds(pl.multiple_of(h * half, half), half)
            res = lax.dot_general(
                conv[:, k, :, lanes].reshape(cols * lat, half),
                mg[R : R + cols].reshape(cols * lat, ch),
                (((0,), (0,)), ((), ())),
                preferred_element_type=F32,
            )
            if not direct:
                mgrad[k, lanes, :] = res
                return
            res = res.reshape(per, 2, 2, rows, ch)
            resb = res.astype(BF16)
            for y in range(2):
                for c in range(2):
                    part[k, c, y, pl.ds(h * per, per)] = res[:, y, c]
                    partb[k, c, y, pl.ds(h * per, per)] = resb[:, y, c]

        loop(0, 2, product)
        if direct:
            core_copy(k).start()
            if k > 0:
                pass_side(k - 1)
        if k == 0:
            turn(sbuf, s_send, s_recv)
    if direct:
        pass_quads(0)
        pass_side(K - 1)

    def spread_grad(g):
        at = pl.ds(4 * g, 4)
        source = mg[at].reshape(4 * lat, ch)
        for k in range(K):
            res = lax.dot_general(
                source, mix[k], (((1,), (1,)), ((), ())), preferred_element_type=F32
            )
            cg[at, k] = res.astype(BF16).reshape(4, lat, ch)

    loop(1, groups, spread_grad)
    grad_l.wait()
    grad_r.wait()
    loop(0, 2, lambda i: spread_grad(i * groups))
    if direct:
        pass_quads(1)

    wait_all(far(sbuf, s_send, s_recv), quads)
    total = jnp.sum(sbuf[4:], axis=0)
    high = total.astype(BF16)
    low = (total - high.astype(F32)).astype(BF16)
    both = jnp.concatenate([high.astype(F32), low.astype(F32)], axis=0).astype(BF16)
    lines = [jnp.zeros((1, ch), F32)] * PB
    for k in range(K):
        res = lax.dot_general(
            both, mix[k], (((1,), (1,)), ((), ())), preferred_element_type=F32
        )
        res = res[0:PB] + res[PB : 2 * PB]
        for i in range(POLAR):
            for q in range(PB):
                lines[q] = lines[q] + (cyc[i, k, q] * scale) * res[i : i + 1]
    lines.append(jnp.zeros((16 - PB, ch), F32))
    zgrad = jnp.concatenate(lines, axis=0)[None]

    def field_group(g):
        at = pl.ds(4 * g, 4)
        source = cg[pl.ds(4 * g, 8)].reshape(8 * K * lat, ch)
        res = jnp.dot(bwd[...], source, preferred_element_type=F32).reshape(4, lat, ch)
        fgrad[at] = res.astype(BF16)
        fgrad[at, 0:16] = (res[:, 0:16] + zgrad).astype(BF16)

    loop(0, groups, field_group)

    if direct:
        pass_quads(K - 1)
        for k in range(K):
            acc = own(k, quad)
            for d in range(1, quads):
                quad_copy(k, d).wait()
                acc = acc + r2[k, d].astype(F32)
            mgrad[k] = acc


def body(n, field, cotangent, offsets, widths, kernel, cycle, mixing):
    lat, cols, ch = field.shape
    scale = float(cols * n) ** (-0.5)
    rows = ch // n
    direct = rows % 16 == 0 and ch % (8 * rows) == 0
    field_t = jnp.swapaxes(field, 0, 1)
    cot_t = jnp.swapaxes(cotangent, 0, 1)
    mix_t = jnp.swapaxes(mixing, 0, 1)
    taps = jnp.transpose(kernel, (2, 3, 1, 0))
    offs = offsets.reshape(1, lat)
    wids = widths.reshape(1, lat)
    cyc = jnp.swapaxes(cycle, 1, 2)

    wide = 2 * K * lat
    dma = pltpu.SemaphoreType.DMA
    quads = n // 4 if direct else 1
    brows = rows if direct else 16
    vmem = pl.BlockSpec(memory_space=pltpu.VMEM)
    hbm = pl.BlockSpec(memory_space=pl.ANY)
    out_t, fgrad_t, mgrad_t = pl.pallas_call(
        functools.partial(kernel_body, n, direct, scale),
        out_shape=[
            jax.ShapeDtypeStruct((cols, lat, ch), BF16),
            jax.ShapeDtypeStruct((cols, lat, ch), BF16),
            jax.ShapeDtypeStruct((K, rows if direct else ch, ch), F32),
        ],
        in_specs=[hbm] * 3 + [vmem] * 3 + [pl.BlockSpec(memory_space=pltpu.SMEM)],
        out_specs=[vmem] * 3,
        scratch_shapes=[
            pltpu.VMEM((cols + 2 * R, lat, ch), BF16),
            pltpu.VMEM((cols, lat, ch), BF16),
            pltpu.VMEM((K, ch, ch), BF16),
            pltpu.VMEM(((TAPS + 1) * lat, wide), F32),
            pltpu.VMEM((wide, (TAPS + 1) * lat), BF16),
            pltpu.VMEM((4 * lat, 4 * wide), BF16),
            pltpu.VMEM((cols, K, lat, ch), BF16),
            pltpu.VMEM((cols, K, 16, ch), F32),
            pltpu.VMEM((cols + 2 * R, lat, ch), BF16),
            pltpu.VMEM((cols + 2 * R, K, lat, ch), BF16),
            pltpu.VMEM((16, ch), F32),
            pltpu.VMEM((4 + n // 4, PB, ch), F32),
            pltpu.VMEM((4 + n // 4, PB, ch), F32),
            pltpu.VMEM((K, 2, 2, quads, brows, ch), F32),
            pltpu.VMEM((K, 2, 2, quads, brows, ch), BF16),
            pltpu.VMEM((K, 2, quads, brows, ch), BF16),
            pltpu.VMEM((K, quads, brows, ch), BF16),
            pltpu.VMEM((K, quads, brows, ch), BF16),
            pltpu.VMEM((K, quads, brows, ch), BF16),
            pltpu.VMEM((K, quads, brows, ch), BF16),
            dma((3,)),
            dma((2,)),
            dma((2,)),
            dma((2,)),
            dma((2,)),
            dma((4 + n // 4,)),
            dma((4 + n // 4,)),
            dma((4 + n // 4,)),
            dma((4 + n // 4,)),
            dma((K,)),
            dma((K,)),
            dma((K,)),
            dma((K,)),
            dma((K, quads)),
            dma((K, quads)),
        ],
        compiler_params=pltpu.CompilerParams(
            collective_id=0, has_side_effects=True, vmem_limit_bytes=36 * 1024 * 1024
        ),
    )(field_t, cot_t, mix_t, taps, offs, wids, cyc)
    output = jnp.swapaxes(out_t, 0, 1)
    field_grad = jnp.swapaxes(fgrad_t, 0, 1)
    mixing_grad = jnp.swapaxes(mgrad_t, 0, 1)
    if not direct:
        mixing_grad = lax.psum_scatter(mixing_grad, "lon", scatter_dimension=0, tiled=True)
    return (output, field_grad, mixing_grad)


def solution(mesh):
    in_specs = (P("grp", "lon", None), P("grp", "lon", None), P(), P(), P(), P(), P())
    out_specs = (P("grp", "lon", None), P("grp", "lon", None), P("lon", "grp", None))
    return jax.shard_map(
        functools.partial(body, mesh.shape["lon"]),
        mesh=mesh,
        in_specs=in_specs,
        out_specs=out_specs,
        check_vma=False,
    )
```
